512 devices in a mesh: video: 4 (over x), patch: 32 (over z, y_lo), head: 4 (over y_hi, core).
Axes of the slice: x: 4, y: 4 (y_hi: 2, y_lo: 2; y = y_hi * 2 + y_lo), z: 16, core: 2. Of those that a mesh axis runs over, the one named last changes fastest.
Arguments:
- fresh_q: bfloat16 [24576, 2560], P(('video', 'patch', 'head')), parts along dimension 0, may hold values from -7 to 7
- fresh_k: bfloat16 [24576, 2560], P(('video', 'patch', 'head')), parts along dimension 0, may hold values from -6.375 to 6.375
- fresh_v: bfloat16 [24576, 2560], P(('video', 'patch', 'head')), parts along dimension 0, may hold values from -4 to 4
- stale_k: bfloat16 [24576, 2560], P(('video', 'patch'), 'head'), parts along dimension 0, may hold values from -26 to 26
- stale_v: bfloat16 [24576, 2560], P(('video', 'patch'), 'head'), parts along dimension 0, may hold values from -16 to 16
- scale_exps: int32 [24576, 2], P(('video', 'patch')), parts along dimension 0, may hold values from -2 to 2, as said below
Outputs:
- attended: bfloat16 [24576, 2560], P(('video', 'patch', 'head')), parts along dimension 0
The draws below stay inside these ranges and needn't reach their ends.
There are 4 independent parts, one for each index of `video`. The reference program is written for one: setup_inputs(seed, part) draws one part's arguments, and reference() takes and returns one part's arrays. A program takes and returns all parts, laid end to end along the dimension named above; each array names one. Nothing has to cross between parts.
Inputs may be any that keep to these rules, and one draw needn't show every extreme that they name: `scale_exps`: column 0 is the exponent for the key row, column 1 for the value row.
All inputs are finite; a program needn't handle non-finite values.
Results may differ from the reference program's by a relative error of at most 0.0055.
Values may be sent and summed in bfloat16 or wider, within the bound.
No kernel may reach another device: no remote copies, remote signals or barrier semaphores. Data moves between devices by JAX's collectives and lax.ppermute only.
A program may use at most 128 MiB of HBM per device.

```python
import math
import jax
import jax.numpy as jnp
from jax import lax

HEADS = 20
HD = 128
TOKENS = 6144
N_PATCH = 32


def shared_exponents(key):
    return jax.random.randint(jax.random.fold_in(key, 11), (TOKENS, 2), -2, 3).astype(jnp.int32)


def draw_scale_exps(key, part):
    return shared_exponents(key)


def draw_fresh_q(key, part):
    key = jax.random.fold_in(key, 1)
    values = 1.6 * jax.random.truncated_normal(key, -4.0, 4.0, (TOKENS, HEADS * HD), jnp.float32)
    return values.astype(jnp.bfloat16)


def draw_stale_k(key, part):
    exponents = shared_exponents(key)[:, 0]
    key = jax.random.fold_in(key, 3)
    values = 1.6 * jax.random.truncated_normal(key, -4.0, 4.0, (TOKENS, HEADS * HD), jnp.float32)
    stored = values * jnp.exp2(-exponents.astype(jnp.float32))[:, None]
    return stored.astype(jnp.bfloat16)


def draw_stale_v(key, part):
    exponents = shared_exponents(key)[:, 1]
    key = jax.random.fold_in(key, 5)
    values = jax.random.truncated_normal(key, -4.0, 4.0, (TOKENS, HEADS * HD), jnp.float32)
    stored = values * jnp.exp2(-exponents.astype(jnp.float32))[:, None]
    return stored.astype(jnp.bfloat16)


def levels(key, dims, cuts, low, top_value):
    factor_of, own = 1.0, jax.random.fold_in(key, 6)
    for axis_at, shards_of in cuts:
        steps = jnp.exp(jax.random.uniform(jax.random.fold_in(own, axis_at), (shards_of,), jnp.float32, low / len(cuts), top_value / len(cuts)))
        factor_of = factor_of * jnp.repeat(steps, dims[axis_at] // shards_of).reshape([-1 if axis == axis_at else 1 for axis in range(len(dims))])
    return factor_of


def centred(rng, dims, deviation, most, split=(), held_as=jnp.bfloat16):
    values = jax.random.normal(rng, dims, jnp.float32) * deviation
    if len(split) > 0:
        values = levels(rng, dims, split, -0.22, 0.18) * values
    return jnp.clip(values, min=-most, max=most).astype(held_as)


def setup_inputs(seed: int = 0, part: int = 0) -> dict:
    key_list = jax.random.split(jax.random.key(seed), 7)
    part_keys = jax.random.split(jax.random.fold_in(key_list[6], part), 7)
    fresh_q = draw_fresh_q(jax.random.fold_in(jax.random.fold_in(key_list[6], part), 71), part)
    fresh_k = centred(part_keys[1], (TOKENS, HEADS * HD), 1.6, 6.375, ((0, 128),))
    fresh_v = centred(part_keys[2], (TOKENS, HEADS * HD), 1.0, 4.0, ((0, 128),))
    stale_k = draw_stale_k(jax.random.fold_in(jax.random.fold_in(key_list[6], part), 71), part)
    stale_v = draw_stale_v(jax.random.fold_in(jax.random.fold_in(key_list[6], part), 71), part)
    scale_exps = draw_scale_exps(jax.random.fold_in(jax.random.fold_in(key_list[6], part), 71), part)
    return dict(fresh_q=fresh_q, fresh_k=fresh_k, fresh_v=fresh_v, stale_k=stale_k, stale_v=stale_v, scale_exps=scale_exps)


def reference(fresh_q, fresh_k, fresh_v, stale_k, stale_v, scale_exps):
    row_width = HEADS * HD
    patch_rows = TOKENS // N_PATCH
    key_scale = jnp.exp2(scale_exps[:, 0].astype(jnp.float32))
    value_scale = jnp.exp2(scale_exps[:, 1].astype(jnp.float32))
    old_keys = (stale_k.astype(jnp.float32) * key_scale[:, None]).astype(jnp.bfloat16)
    old_values = (stale_v.astype(jnp.float32) * value_scale[:, None]).astype(jnp.bfloat16)
    factor = 1.0 / math.sqrt(HD)

    def one_patch(patch_number):
        lower = (patch_number * patch_rows).astype(jnp.int32)
        queries = lax.dynamic_slice_in_dim(fresh_q, lower, patch_rows, 0)
        own_keys = lax.dynamic_slice_in_dim(fresh_k, lower, patch_rows, 0)
        own_values = lax.dynamic_slice_in_dim(fresh_v, lower, patch_rows, 0)
        all_keys = lax.dynamic_update_slice_in_dim(old_keys, own_keys, lower, 0)
        all_values = lax.dynamic_update_slice_in_dim(old_values, own_values, lower, 0)
        query_heads = queries.astype(jnp.float32).reshape(patch_rows, HEADS, HD)
        key_heads = all_keys.astype(jnp.float32).reshape(TOKENS, HEADS, HD)
        value_heads = all_values.astype(jnp.float32).reshape(TOKENS, HEADS, HD)
        scores = jnp.einsum('rhd,khd->rhk', query_heads, key_heads) * factor
        highest = lax.optimization_barrier(jnp.max(scores, axis=-1, keepdims=True))
        expon = jnp.exp(scores - highest)
        total = lax.optimization_barrier(jnp.sum(expon, axis=-1))
        rounded = lax.optimization_barrier(expon.astype(jnp.bfloat16))
        mixed = jnp.einsum('rhk,khd->rhd', rounded.astype(jnp.float32), value_heads)
        result = mixed / total[:, :, None]
        return result.reshape(patch_rows, row_width).astype(jnp.bfloat16)
    stacked = lax.map(one_patch, jnp.arange(N_PATCH, dtype=jnp.int32))
    return stacked.reshape(TOKENS, row_width)
```

```python
import functools
import math

import jax
import jax.numpy as jnp
import numpy as np
from jax import lax
from jax.experimental import pallas as pl
from jax.experimental.pallas import tpu as pltpu
from jax.sharding import Mesh, PartitionSpec as P


HD = 128
LOG2_SCALE = math.log2(math.e) / math.sqrt(HD)
LOWEST = -1e30
SUB = 48
PATCH = 192
PACKED = 64
VMEM_BYTES = 40 * 2**20
VM = pl.BlockSpec(memory_space=pltpu.VMEM)
SM = pl.BlockSpec(memory_space=pltpu.SMEM)
BF16, F32 = jnp.bfloat16, jnp.float32
CHUNKS = ((0, 1), (2, 3))
STEPS_Y = (0, 1, 3, 2)


def call(kernel, name, outs, in_specs):
    return pl.pallas_call(
        kernel,
        out_shape=outs,
        in_specs=in_specs,
        out_specs=[VM] * len(outs),
        compiler_params=pltpu.CompilerParams(vmem_limit_bytes=VMEM_BYTES),
        name=name,
    )


def prepare_kernel(first_ref, k_ref, v_ref, exps_ref, q_ref, fk_ref, fv_ref, *outs):
    rounds, line_ref, q_plane_ref, q_line_ref, fresh_ref = outs[:4], *outs[4:]
    scales = jnp.exp2(exps_ref[...].astype(F32))
    k_scale, v_scale = scales[:, 0:1], scales[:, 1:2]

    def pair(column):
        k = k_ref[:, pl.ds(column, HD)].astype(F32) * k_scale
        v = v_ref[:, pl.ds(column, HD)].astype(F32) * v_scale
        return k.astype(BF16), v.astype(BF16)

    for r in range(4):
        j = (first_ref[0] + r) % 4
        k, v = pair(pl.multiple_of(j * HD, HD))
        rounds[r][:, :HD] = k
        rounds[r][:, HD:] = v
    k, v = pair(4 * HD)
    line_ref[:, :HD] = k
    line_ref[:, HD:] = v
    for g in range(4):
        for j in range(4):
            at = (5 * g + j) * HD
            q_plane_ref[4 * j + g] = q_ref[:, at : at + HD]
        at = (5 * g + 4) * HD
        q_line_ref[g] = q_ref[:, at : at + HD]
        q_line_ref[4 + g] = q_ref[:, at : at + HD]
    width = fk_ref.shape[1]
    fresh_ref[:, :width] = fk_ref[...]
    fresh_ref[:, width:] = fv_ref[...]


def attend_kernel(group, has_state, last, n_kv, *refs):
    spans_ref, q_ref = refs[:2]
    kv_refs = refs[2 : 2 + n_kv]
    rest = refs[2 + n_kv :]
    queries = q_ref[...]
    count = queries.shape[0]
    lanes = lax.broadcasted_iota(jnp.int32, (1, count), 1)
    keys = group * PATCH

    if has_state:
        state = tuple(ref[...] for ref in rest[:3])
        rest = rest[3:]
    else:
        state = (
            jnp.full((1, count), LOWEST, F32),
            jnp.zeros((1, count), F32),
            jnp.zeros((HD, count), F32),
        )
    patch = 0
    for kv_ref in kv_refs:

        def step(i, state, kv_ref=kv_ref, patch=patch):
            top, total, acc = state
            rows = pl.ds(pl.multiple_of(i * keys, keys), keys)
            k, v = kv_ref[rows, :HD], kv_ref[rows, HD:]
            s = lax.dot_general(k, queries, (((1,), (1,)), ((), ())), preferred_element_type=F32)
            blocks, masks = [], []
            new_top = top
            for n in range(group):
                block = s[n * PATCH : (n + 1) * PATCH]
                at = patch + i * group + n
                mask = (lanes >= spans_ref[at, 0]) & (lanes < spans_ref[at, 1])
                block_top = jnp.max(block, axis=0, keepdims=True)
                new_top = jnp.maximum(new_top, jnp.where(mask, LOWEST, block_top))
                blocks.append(block)
                masks.append(mask)
            shift = new_top * LOG2_SCALE
            weights = []
            shrink = jnp.exp2(top * LOG2_SCALE - shift)
            total = total * shrink
            for block, mask in zip(blocks, masks):
                w = jnp.exp2(block * LOG2_SCALE - jnp.where(mask, -LOWEST, shift))
                total = total + jnp.sum(w, axis=0, keepdims=True)
                weights.append(w.astype(BF16))
            w = jnp.concatenate(weights, axis=0)
            acc = acc * shrink + lax.dot_general(
                v, w, (((0,), (0,)), ((), ())), preferred_element_type=F32
            )
            return new_top, total, acc

        steps = kv_ref.shape[0] // keys
        state = lax.fori_loop(0, steps, step, state)
        patch += steps * group

    if not last:
        for ref, value in zip(rest, state):
            ref[...] = value
        return
    (out_ref,) = rest
    top, total, acc = state
    result = (acc / total).T.astype(BF16)
    log_sum = top * LOG2_SCALE + jnp.log2(total)
    high = log_sum.astype(BF16).astype(F32)
    middle = (log_sum - high).astype(BF16).astype(F32)
    low = log_sum - high - middle
    parts = jnp.concatenate([high, middle, low, jnp.zeros((13, count), F32)], axis=0)
    for n in range(count // SUB):
        out_ref[n, :SUB] = result[n * SUB : (n + 1) * SUB]
        moved = parts if n == 0 else pltpu.roll(parts, count - n * SUB, 1)
        out_ref[n, SUB:] = moved[:, :HD].astype(BF16)


def attend(name, spans, q, kvs, group, state=None, last=True):
    count = q.shape[0]
    if last:
        outs = [jax.ShapeDtypeStruct((count // SUB, PACKED, HD), BF16)]
    else:
        outs = [
            jax.ShapeDtypeStruct((1, count), F32),
            jax.ShapeDtypeStruct((1, count), F32),
            jax.ShapeDtypeStruct((HD, count), F32),
        ]
    kernel = functools.partial(attend_kernel, group, state is not None, last, len(kvs))
    state = () if state is None else tuple(state)
    specs = [SM] + [VM] * (1 + len(kvs) + len(state))
    return call(kernel, name, outs, specs)(spans, q, *kvs, *state)


def plane_order(h):
    g, j = h // 5, h % 5
    return 16 + g if j == 4 else 4 * j + g


def fresh_kernel(q_ref, kv_ref, out_ref, log_ref):
    width = q_ref.shape[1]
    lanes = lax.broadcasted_iota(jnp.int32, (SUB, HD), 1)
    logs = jnp.zeros((SUB, HD), F32)
    for h in range(width // HD):
        at = h * HD
        q = q_ref[:, at : at + HD]
        k = kv_ref[:, at : at + HD]
        v = kv_ref[:, width + at : width + at + HD]
        s = lax.dot_general(q, k, (((1,), (1,)), ((), ())), preferred_element_type=F32)
        top = jnp.max(s, axis=1, keepdims=True)
        w = jnp.exp2((s - top) * LOG2_SCALE)
        total = jnp.sum(w, axis=1, keepdims=True)
        out_ref[:, at : at + HD] = (
            jnp.dot(w.astype(BF16), v, preferred_element_type=F32) / total
        )
        logs = jnp.where(lanes == plane_order(h), top * LOG2_SCALE + jnp.log2(total), logs)
    log_ref[...] = logs


def merge_kernel(plane_ref, line_ref, fresh_ref, fresh_log_ref, out_ref):
    def logs_of(ref):
        rows = jnp.sum(ref[:, SUB:, :].astype(F32), axis=1)
        return rows.T[:SUB]

    plane_log, line_log = logs_of(plane_ref), logs_of(line_ref)
    fresh_log = fresh_log_ref[...]
    fresh_plane, fresh_line = fresh_log[:, :16], fresh_log[:, 16:20]
    line_a, line_b = line_log[:, :4], line_log[:, 4:]

    top = jnp.maximum(plane_log, fresh_plane)
    a, b = jnp.exp2(plane_log - top), jnp.exp2(fresh_plane - top)
    scale = 1.0 / (a + b)
    a, b = a * scale, b * scale
    top = jnp.maximum(jnp.maximum(line_a, line_b), fresh_line)
    la, lb, lf = (jnp.exp2(value - top) for value in (line_a, line_b, fresh_line))
    scale = 1.0 / (la + lb + lf)
    la, lb, lf = la * scale, lb * scale, lf * scale
    for h in range(20):
        at = h * HD
        fresh = fresh_ref[:, at : at + HD]
        n = plane_order(h)
        if n < 16:
            value = a[:, n : n + 1] * plane_ref[n, :SUB].astype(F32) + b[:, n : n + 1] * fresh
        else:
            g = n - 16
            value = (
                la[:, g : g + 1] * line_ref[g, :SUB].astype(F32)
                + lb[:, g : g + 1] * line_ref[4 + g, :SUB].astype(F32)
                + lf[:, g : g + 1] * fresh
            )
        out_ref[:, at : at + HD] = value.astype(BF16)


def round_pairs(r, planes):
    pairs = []
    for z in range(planes):
        for yl in range(2):
            for g in range(4):
                target = 4 * ((z % 4 + r) % 4) + g
                pairs.append(((z * 2 + yl) * 4 + g, (target * 2 + yl) * 4 + z // 4))
    return pairs


def step_pairs(dy):
    pairs = []
    for y in range(4):
        t = (y + dy) % 4
        pairs.append(((y % 2) * 2 + y // 2, (t % 2) * 2 + t // 2))
    return pairs


def per_device(fresh_q, fresh_k, fresh_v, stale_k, stale_v, scale_exps):
    z, yl, yh, c = (lax.axis_index(name) for name in ("z", "yl", "yh", "c"))
    shape = jax.ShapeDtypeStruct
    prepared = call(
        prepare_kernel,
        "prepare",
        [shape((PATCH, 2 * HD), BF16)] * 5
        + [
            shape((16, SUB, HD), BF16),
            shape((8, SUB, HD), BF16),
            shape((SUB, 2 * fresh_k.shape[1]), BF16),
        ],
        [SM] + [VM] * 6,
    )((z % 4).reshape(1), stale_k, stale_v, scale_exps, fresh_q, fresh_k, fresh_v)
    rounds, kv_line, q_plane, q_line, fresh_kv = prepared[:4], *prepared[4:]

    arrived = [
        lax.ppermute(rounds[r], ("z", "yl", "yh", "c"), round_pairs(r, 16)) for r in range(4)
    ]
    q_plane = lax.all_to_all(q_plane, "z", split_axis=0, concat_axis=0, tiled=True)
    q_plane = q_plane.reshape(16 * SUB, HD)
    q_line = lax.all_to_all(q_line, ("yl", "yh", "c"), split_axis=0, concat_axis=0, tiled=True)
    q_line = q_line.reshape(8 * SUB, HD)
    kv_line = lax.all_gather(kv_line, "z", axis=0, tiled=True)
    fresh_kv = lax.all_gather(fresh_kv, ("yh", "c"), axis=0, tiled=True)

    fresh, fresh_log = call(
        fresh_kernel,
        "own_patch",
        [shape(fresh_q.shape, F32), shape((SUB, HD), F32)],
        [VM] * 2,
    )(fresh_q, fresh_kv)

    own = jnp.arange(16, dtype=jnp.int32) == z
    low = jnp.where(own, PATCH * yl, -1)
    spans = jnp.stack([low, jnp.where(own, low + PATCH, -1)], axis=1)
    (line,) = attend("line_heads", spans, q_line, [kv_line], 8)
    line = lax.all_to_all(line, ("yl", "yh", "c"), split_axis=0, concat_axis=0, tiled=True)

    j = z // 4
    y = 2 * yh + yl
    state = None
    for chunk in CHUNKS:
        shard = jnp.concatenate([arrived[r] for r in chunk], axis=0)
        same = jnp.concatenate(
            [shard if dy == 0 else lax.ppermute(shard, ("yl", "yh"), step_pairs(dy)) for dy in STEPS_Y],
            axis=0,
        )
        other = lax.ppermute(same, "c", [(0, 1), (1, 0)])
        lows = []
        for core in (c, 1 - c):
            for dy in STEPS_Y:
                source = (y + 4 - dy) % 4
                for r in chunk:
                    patch = 4 * ((source // 2) * 2 + core) + (j + 4 - r) % 4
                    lows.append(SUB * patch if dy % 2 == 0 else jnp.int32(-SUB))
        low = jnp.stack([value.astype(jnp.int32) for value in lows])
        spans = jnp.stack([low, low + SUB], axis=1)
        last = chunk == CHUNKS[-1]
        state = attend(
            "plane_heads_last" if last else "plane_heads", spans, q_plane, [same, other], 8, state, last
        )
    (plane,) = state
    plane = lax.all_to_all(plane, "z", split_axis=0, concat_axis=0, tiled=True)

    (out,) = call(merge_kernel, "merge", [shape(fresh_q.shape, BF16)], [VM] * 4)(
        plane, line, fresh, fresh_log
    )
    return out


def solution(mesh):
    devices = np.asarray(mesh.devices).reshape(4, 16, 2, 2, 2)
    fine = Mesh(devices, ("x", "z", "yl", "yh", "c"))
    tokens = P(("x", "z", "yl", "yh", "c"), None)
    stored = P(("x", "z", "yl"), ("yh", "c"))
    in_specs = (tokens, tokens, tokens, stored, stored, P(("x", "z", "yl"), None))
    return jax.shard_map(
        per_device, mesh=fine, in_specs=in_specs, out_specs=tokens, check_vma=False
    )
```

```python
import functools
import math

import jax
import jax.numpy as jnp
import numpy as np
from jax import lax
from jax.experimental import pallas as pl
from jax.experimental.pallas import tpu as pltpu
from jax.sharding import Mesh, PartitionSpec as P


HD = 128
LOG2_SCALE = math.log2(math.e) / math.sqrt(HD)
LOWEST = -1e30
SUB = 48
PATCH = 192
PACKED = 112
VMEM_BYTES = 24 * 2**20
VM = pl.BlockSpec(memory_space=pltpu.VMEM)
SM = pl.BlockSpec(memory_space=pltpu.SMEM)
BF16, F32 = jnp.bfloat16, jnp.float32


def call(kernel, name, outs, in_specs):
    return pl.pallas_call(
        kernel,
        out_shape=outs,
        in_specs=in_specs,
        out_specs=[VM] * len(outs),
        compiler_params=pltpu.CompilerParams(vmem_limit_bytes=VMEM_BYTES),
        name=name,
    )


def stored_kernel(first_ref, k_ref, v_ref, exps_ref, *rounds):
    scales = jnp.exp2(exps_ref[...].astype(F32))
    scales = jnp.concatenate([scales, jnp.zeros((6, PATCH), F32)], axis=0).T
    k_scale, v_scale = scales[:, 0:1], scales[:, 1:2]

    def put(ref, row, column):
        k = k_ref[:, pl.ds(column, HD)].astype(F32) * k_scale
        v = v_ref[:, pl.ds(column, HD)].astype(F32) * v_scale
        ref[row : row + PATCH, :HD] = k.astype(BF16)
        ref[row : row + PATCH, HD:] = v.astype(BF16)

    for r in range(4):
        j = (first_ref[0] + r * first_ref[1]) % 4
        put(rounds[r], 0, pl.multiple_of(j * HD, HD))
    put(rounds[0], PATCH, 4 * HD)


def fresh_layout_kernel(q_ref, fk_ref, fv_ref, q_out_ref, fresh_ref):
    for g in range(4):
        for j in range(4):
            at = (5 * g + j) * HD
            q_out_ref[4 * j + g, :SUB] = q_ref[:, at : at + HD]
            at = (5 * g + 4) * HD
            q_out_ref[4 * j + g, SUB:] = q_ref[:, at : at + HD]
    width = fk_ref.shape[1]
    fresh_ref[:, :width] = fk_ref[...]
    fresh_ref[:, width:] = fv_ref[...]


def start_state(count):
    return (
        jnp.full((1, count), LOWEST, F32),
        jnp.zeros((1, count), F32),
        jnp.zeros((HD, count), F32),
    )


def accumulate(state, queries, kv_refs, spans_ref, groups):
    top, total, acc = state
    lanes = lax.broadcasted_iota(jnp.int32, (1, queries.shape[0]), 1)
    for group in groups:
        k = jnp.concatenate([kv_refs[n][row : row + PATCH, :HD] for n, row, _ in group], axis=0)
        v = jnp.concatenate([kv_refs[n][row : row + PATCH, HD:] for n, row, _ in group], axis=0)
        s = lax.dot_general(k, queries, (((1,), (1,)), ((), ())), preferred_element_type=F32)
        blocks, masks = [], []
        new_top = top
        for n, (_, _, span) in enumerate(group):
            block = s[n * PATCH : (n + 1) * PATCH]
            low = spans_ref[span]
            mask = (lanes >= low) & (lanes < low + SUB)
            block_top = jnp.max(block, axis=0, keepdims=True)
            new_top = jnp.maximum(new_top, jnp.where(mask, LOWEST, block_top))
            blocks.append(block)
            masks.append(mask)
        shift = new_top * LOG2_SCALE
        weights = []
        shrink = jnp.exp2(top * LOG2_SCALE - shift)
        total = total * shrink
        for block, mask in zip(blocks, masks):
            w = jnp.exp2(block * LOG2_SCALE - jnp.where(mask, -LOWEST, shift))
            total = total + jnp.sum(w, axis=0, keepdims=True)
            weights.append(w.astype(BF16))
        w = jnp.concatenate(weights, axis=0)
        acc = acc * shrink + lax.dot_general(
            v, w, (((0,), (0,)), ((), ())), preferred_element_type=F32
        )
        top = new_top
    return top, total, acc


def finish(state):
    top, total, acc = state
    log_sum = top * LOG2_SCALE + jnp.log2(total)
    high = log_sum.astype(BF16).astype(F32)
    middle = (log_sum - high).astype(BF16).astype(F32)
    return (acc / total).T.astype(BF16), [high, middle, log_sum - high - middle]


def queries_of(q_ref):
    count = q_ref.shape[0] * SUB
    return q_ref[:, :SUB].reshape(count, HD), q_ref[:, SUB:].reshape(count, HD)


def attend_kernel(groups, n_kv, has_state, last, spans_ref, q_ref, *refs):
    kv_refs, refs = refs[:n_kv], refs[n_kv:]
    results, rows = [], []
    for n, queries in enumerate(queries_of(q_ref)):
        if has_state:
            state = tuple(ref[...] for ref in refs[3 * n : 3 * n + 3])
        else:
            state = start_state(queries.shape[0])
        state = accumulate(state, queries, kv_refs, spans_ref, groups[n])
        if last:
            result, log_rows = finish(state)
            results.append(result)
            rows += log_rows
        else:
            for ref, value in zip(refs[6 * has_state + 3 * n :], state):
                ref[...] = value
    if not last:
        return
    out_ref = refs[-1]
    count = results[0].shape[0]
    rows = jnp.concatenate(rows + [jnp.zeros((10, count), F32)], axis=0)
    for n in range(count // SUB):
        out_ref[n, :SUB] = results[0][n * SUB : (n + 1) * SUB]
        out_ref[n, SUB : 2 * SUB] = results[1][n * SUB : (n + 1) * SUB]
        moved = rows if n == 0 else pltpu.roll(rows, count - n * SUB, 1)
        out_ref[n, 2 * SUB :] = moved[:, :HD].astype(BF16)


def attend(name, spans, q, shards, state=None, last=False):
    arrays = []
    for array, _, _ in shards:
        if not any(array is other for other in arrays):
            arrays.append(array)
    main, extra = [], []
    for array, row, span in shards:
        at = [n for n, other in enumerate(arrays) if other is array][0]
        main += [(at, row + (r + 1 if r else 0) * PATCH, span + r) for r in range(4)]
        extra.append((at, row + PATCH, span))
    groups = ([main[n : n + 8] for n in range(0, len(main), 8)], [extra])
    count = q.shape[0] * SUB
    shape = jax.ShapeDtypeStruct
    outs = [shape((1, count), F32), shape((1, count), F32), shape((HD, count), F32)] * 2
    if last:
        outs = [shape((q.shape[0], PACKED, HD), BF16)]
    state = () if state is None else tuple(state)
    kernel = functools.partial(attend_kernel, groups, len(arrays), bool(state), last)
    specs = [SM] + [VM] * (1 + len(arrays) + len(state))
    return call(kernel, name, outs, specs)(spans, q, *arrays, *state)


def plane_order(h):
    g, j = h // 5, h % 5
    return 16 + g if j == 4 else 4 * j + g


def fresh_kernel(q_ref, near_ref, far_ref, out_ref, log_ref):
    kv_refs = (near_ref, far_ref)
    width = q_ref.shape[1]
    lanes = lax.broadcasted_iota(jnp.int32, (SUB, HD), 1)
    logs = jnp.zeros((SUB, HD), F32)
    for h in range(width // HD):
        at = h * HD
        q = q_ref[:, at : at + HD]
        k = jnp.concatenate([ref[:, at : at + HD] for ref in kv_refs], axis=0)
        v = jnp.concatenate([ref[:, width + at : width + at + HD] for ref in kv_refs], axis=0)
        s = lax.dot_general(q, k, (((1,), (1,)), ((), ())), preferred_element_type=F32)
        top = jnp.max(s, axis=1, keepdims=True)
        w = jnp.exp2((s - top) * LOG2_SCALE)
        total = jnp.sum(w, axis=1, keepdims=True)
        out_ref[:, at : at + HD] = (
            jnp.dot(w.astype(BF16), v, preferred_element_type=F32) / total
        )
        logs = jnp.where(lanes == plane_order(h), top * LOG2_SCALE + jnp.log2(total), logs)
    log_ref[...] = logs


def merge_kernel(both_ref, fresh_ref, fresh_log_ref, out_ref):
    main_ref, extra_ref = both_ref.at[:, :SUB], both_ref.at[:, SUB : 2 * SUB]
    rows = both_ref[:, 2 * SUB :].astype(F32)
    main_log = jnp.sum(rows[:, 0:3], axis=1).T[:SUB]
    extra_log = jnp.sum(rows[:, 3:6], axis=1).T[:SUB]
    fresh_log = fresh_log_ref[...]
    fresh_main, fresh_extra = fresh_log[:, :16], fresh_log[:, 16:20]

    top = jnp.maximum(main_log, fresh_main)
    a, b = jnp.exp2(main_log - top), jnp.exp2(fresh_main - top)
    scale = 1.0 / (a + b)
    a, b = a * scale, b * scale
    parts = [extra_log[:, 4 * j : 4 * j + 4] for j in range(4)] + [fresh_extra]
    top = functools.reduce(jnp.maximum, parts)
    parts = [jnp.exp2(part - top) for part in parts]
    scale = 1.0 / functools.reduce(jnp.add, parts)
    parts = [part * scale for part in parts]
    for h in range(20):
        at = h * HD
        fresh = fresh_ref[:, at : at + HD]
        n = plane_order(h)
        if n < 16:
            value = a[:, n : n + 1] * main_ref[n].astype(F32) + b[:, n : n + 1] * fresh
        else:
            g = n - 16
            value = parts[4][:, g : g + 1] * fresh
            for j in range(4):
                value += parts[j][:, g : g + 1] * extra_ref[4 * j + g].astype(F32)
        out_ref[:, at : at + HD] = value.astype(BF16)


def round_pairs(r):
    pairs = []
    for z in range(16):
        for yl in range(2):
            for yh in range(2):
                for c in range(2):
                    g, move = yh * 2 + c, (z // 2 % 2) ^ c
                    plane = 4 * ((z // 4 + (r if c == 0 else 4 - r)) % 4) + g
                    target = ((plane * 2 + (yl ^ move)) * 2 + (yh ^ move)) * 2 + z % 2
                    pairs.append(((z * 2 + yl) * 4 + g, target))
    return pairs


def per_device(fresh_q, fresh_k, fresh_v, stale_k, stale_v, scale_exps):
    z, yl, yh, c = (lax.axis_index(name) for name in ("z", "yl", "yh", "c"))
    shape = jax.ShapeDtypeStruct
    j = z // 4

    rounds = call(
        stored_kernel,
        "stored_scaled",
        [shape((PATCH * (2 if r == 0 else 1), 2 * HD), BF16) for r in range(4)],
        [SM] + [VM] * 3,
    )(jnp.stack([j, 1 + 2 * c]).astype(jnp.int32), stale_k, stale_v, scale_exps.T)
    arrived = [
        lax.ppermute(rounds[r], ("z", "yl", "yh", "c"), round_pairs(r)) for r in range(4)
    ]
    q, fresh_kv = call(
        fresh_layout_kernel,
        "fresh_layout",
        [shape((16, 2 * SUB, HD), BF16), shape((SUB, 2 * fresh_k.shape[1]), BF16)],
        [VM] * 3,
    )(fresh_q, fresh_k, fresh_v)
    arrived, q = lax.optimization_barrier((arrived, q))
    q = lax.all_to_all(q, "z", split_axis=0, concat_axis=0, tiled=True)

    shard = jnp.concatenate(arrived, axis=0)
    swap = [(0, 1), (1, 0)]
    parts = [shard] + [
        lax.ppermute(shard, ("yl", "yh"), [(i, i ^ k) for i in range(4)]) for k in (1, 2, 3)
    ]
    across_0 = lax.ppermute(shard, "c", swap)
    across_2 = lax.ppermute(parts[2], "c", swap)
    across_13 = lax.ppermute(jnp.concatenate([parts[1], parts[3]], axis=0), "c", swap)
    lows = []
    for core in (c, 1 - c):
        for k in range(4):
            source_yl, source_yh = yl ^ (k // 2), yh ^ (k % 2)
            move = source_yh ^ (z // 2 % 2)
            for r in range(4):
                patch = 4 * ((j + (4 - r) * (1 + 2 * (z % 2))) % 4) + 2 * (move ^ (z % 2)) + core
                lows.append(jnp.where(source_yl ^ move == yl, SUB * patch, -SUB))
    spans = jnp.stack([low.astype(jnp.int32) for low in lows])

    fresh_kv, parts[1], parts[3] = lax.optimization_barrier((fresh_kv, parts[1], parts[3]))
    fresh_far = lax.ppermute(fresh_kv, "yh", swap)
    rows = shard.shape[0]
    state = attend("keys_a", spans, q, [(shard, 0, 0), (across_0, 0, 16)])
    state = attend("keys_b", spans, q, [(parts[2], 0, 8), (across_2, 0, 24)], state)
    state = attend("keys_c", spans, q, [(parts[1], 0, 4), (parts[3], 0, 12)], state)
    (both,) = attend(
        "keys_d", spans, q, [(across_13, 0, 20), (across_13, rows, 28)], state, True
    )
    both = lax.all_to_all(both, "z", split_axis=0, concat_axis=0, tiled=True)

    fresh_two = jnp.concatenate([fresh_kv, fresh_far], axis=0)
    fresh, fresh_log = call(
        fresh_kernel,
        "own_patch",
        [shape(fresh_q.shape, F32), shape((SUB, HD), F32)],
        [VM] * 3,
    )(fresh_q, fresh_two, lax.ppermute(fresh_two, "c", [(0, 1), (1, 0)]))

    (out,) = call(merge_kernel, "merge", [shape(fresh_q.shape, BF16)], [VM] * 3)(
        both, fresh, fresh_log
    )
    return out


def solution(mesh):
    devices = np.asarray(mesh.devices).reshape(4, 16, 2, 2, 2)
    fine = Mesh(devices, ("x", "z", "yl", "yh", "c"))
    tokens = P(("x", "z", "yl", "yh", "c"), None)
    stored = P(("x", "z", "yl"), ("yh", "c"))
    in_specs = (tokens, tokens, tokens, stored, stored, P(("x", "z", "yl"), None))
    return jax.shard_map(
        per_device, mesh=fine, in_specs=in_specs, out_specs=tokens, check_vma=False
    )
```

```python
import functools
import math

import jax
import jax.numpy as jnp
import numpy as np
from jax import lax
from jax.experimental import pallas as pl
from jax.experimental.pallas import tpu as pltpu
from jax.sharding import Mesh, PartitionSpec as P


HD = 128
LOG2_SCALE = math.log2(math.e) / math.sqrt(HD)
LOWEST = -1e30
SUB = 48
PATCH = 192
PACKED = 112
VMEM_BYTES = 24 * 2**20
VM = pl.BlockSpec(memory_space=pltpu.VMEM)
SM = pl.BlockSpec(memory_space=pltpu.SMEM)
BF16, F32 = jnp.bfloat16, jnp.float32


def call(kernel, name, outs, in_specs):
    return pl.pallas_call(
        kernel,
        out_shape=outs,
        in_specs=in_specs,
        out_specs=[VM] * len(outs),
        compiler_params=pltpu.CompilerParams(vmem_limit_bytes=VMEM_BYTES),
        name=name,
    )


def stored_kernel(first_ref, k_ref, v_ref, exps_ref, *rounds):
    scales = jnp.exp2(exps_ref[...].astype(F32))
    scales = jnp.concatenate([scales, jnp.zeros((6, PATCH), F32)], axis=0).T
    k_scale, v_scale = scales[:, 0:1], scales[:, 1:2]

    def put(ref, row, column):
        k = k_ref[:, pl.ds(column, HD)].astype(F32) * k_scale
        v = v_ref[:, pl.ds(column, HD)].astype(F32) * v_scale
        ref[row : row + PATCH, :HD] = k.astype(BF16)
        ref[row : row + PATCH, HD:] = v.astype(BF16)

    for r in range(4):
        j = (first_ref[0] + r * first_ref[1]) % 4
        put(rounds[r], 0, pl.multiple_of(j * HD, HD))
    put(rounds[0], PATCH, 4 * HD)


def fresh_layout_kernel(q_ref, fk_ref, fv_ref, q_out_ref, fresh_ref):
    for g in range(4):
        for j in range(4):
            at = (5 * g + j) * HD
            q_out_ref[4 * j + g, :SUB] = q_ref[:, at : at + HD]
            at = (5 * g + 4) * HD
            q_out_ref[4 * j + g, SUB:] = q_ref[:, at : at + HD]
    width = fk_ref.shape[1]
    fresh_ref[:, :width] = fk_ref[...]
    fresh_ref[:, width:] = fv_ref[...]


def start_state(count):
    return (
        jnp.full((1, count), LOWEST, F32),
        jnp.zeros((1, count), F32),
        jnp.zeros((HD, count), F32),
    )


def accumulate(state, queries, kv_refs, spans_ref, groups):
    top, total, acc = state
    lanes = lax.broadcasted_iota(jnp.int32, (1, queries.shape[0]), 1)
    for group in groups:
        k = jnp.concatenate([kv_refs[n][row : row + PATCH, :HD] for n, row, _ in group], axis=0)
        v = jnp.concatenate([kv_refs[n][row : row + PATCH, HD:] for n, row, _ in group], axis=0)
        s = lax.dot_general(k, queries, (((1,), (1,)), ((), ())), preferred_element_type=F32)
        blocks, masks = [], []
        new_top = top
        for n, (_, _, span) in enumerate(group):
            block = s[n * PATCH : (n + 1) * PATCH]
            low = spans_ref[span]
            mask = (lanes >= low) & (lanes < low + SUB)
            block_top = jnp.max(block, axis=0, keepdims=True)
            new_top = jnp.maximum(new_top, jnp.where(mask, LOWEST, block_top))
            blocks.append(block)
            masks.append(mask)
        shift = new_top * LOG2_SCALE
        weights = []
        shrink = jnp.exp2(top * LOG2_SCALE - shift)
        total = total * shrink
        for block, mask in zip(blocks, masks):
            w = jnp.exp2(block * LOG2_SCALE - jnp.where(mask, -LOWEST, shift))
            total = total + jnp.sum(w, axis=0, keepdims=True)
            weights.append(w.astype(BF16))
        w = jnp.concatenate(weights, axis=0)
        acc = acc * shrink + lax.dot_general(
            v, w, (((0,), (0,)), ((), ())), preferred_element_type=F32
        )
        top = new_top
    return top, total, acc


def finish(state):
    top, total, acc = state
    log_sum = top * LOG2_SCALE + jnp.log2(total)
    high = log_sum.astype(BF16).astype(F32)
    middle = (log_sum - high).astype(BF16).astype(F32)
    return (acc * (1.0 / total)).T.astype(BF16), [high, middle, log_sum - high - middle]


def queries_of(q_ref):
    count = q_ref.shape[0] * SUB
    return q_ref[:, :SUB].reshape(count, HD), q_ref[:, SUB:].reshape(count, HD)


def attend_kernel(groups, n_kv, has_state, last, spans_ref, q_ref, *refs):
    kv_refs, refs = refs[:n_kv], refs[n_kv:]
    results, rows = [], []
    for n, queries in enumerate(queries_of(q_ref)):
        if has_state:
            state = tuple(ref[...] for ref in refs[3 * n : 3 * n + 3])
        else:
            state = start_state(queries.shape[0])
        state = accumulate(state, queries, kv_refs, spans_ref, groups[n])
        if last:
            result, log_rows = finish(state)
            results.append(result)
            rows += log_rows
        else:
            for ref, value in zip(refs[6 * has_state + 3 * n :], state):
                ref[...] = value
    if not last:
        return
    out_ref = refs[-1]
    count = results[0].shape[0]
    rows = jnp.concatenate(rows + [jnp.zeros((2, count), F32)], axis=0)
    empty = jnp.zeros((8, HD), F32)
    for n in range(count // SUB):
        out_ref[n, :SUB] = results[0][n * SUB : (n + 1) * SUB]
        out_ref[n, SUB : 2 * SUB] = results[1][n * SUB : (n + 1) * SUB]
        low = min(n * SUB // HD * HD, count - 2 * HD)
        moved = rows[:, low : low + 2 * HD]
        if n * SUB > low:
            moved = pltpu.roll(moved, 2 * HD - (n * SUB - low), 1)
        moved = jnp.concatenate([moved[:, :HD], empty], axis=0)
        out_ref[n, 2 * SUB :] = moved.astype(BF16)


def attend(name, spans, q, shards, state=None, last=False):
    arrays = []
    for array, _, _ in shards:
        if not any(array is other for other in arrays):
            arrays.append(array)
    main, extra = [], []
    for array, row, span in shards:
        at = [n for n, other in enumerate(arrays) if other is array][0]
        main += [(at, row + (r + 1 if r else 0) * PATCH, span + r) for r in range(4)]
        extra.append((at, row + PATCH, span))
    groups = ([main[n : n + 8] for n in range(0, len(main), 8)], [extra])
    count = q.shape[0] * SUB
    shape = jax.ShapeDtypeStruct
    outs = [shape((1, count), F32), shape((1, count), F32), shape((HD, count), F32)] * 2
    if last:
        outs = [shape((q.shape[0], PACKED, HD), BF16)]
    state = () if state is None else tuple(state)
    kernel = functools.partial(attend_kernel, groups, len(arrays), bool(state), last)
    specs = [SM] + [VM] * (1 + len(arrays) + len(state))
    return call(kernel, name, outs, specs)(spans, q, *arrays, *state)


def plane_order(h):
    g, j = h // 5, h % 5
    return 16 + g if j == 4 else 4 * j + g


def fresh_kernel(q_ref, near_ref, far_ref, out_ref, log_ref):
    width = q_ref.shape[1]
    lanes = lax.broadcasted_iota(jnp.int32, (SUB, HD), 1)
    tops, totals = jnp.zeros((SUB, HD), F32), jnp.ones((SUB, HD), F32)
    both = (near_ref, far_ref)
    for first in range(0, width // HD, 10):
        heads = range(first, first + 10)
        scores, weights = [], []
        for h in heads:
            at = h * HD
            k = jnp.concatenate([ref[:, at : at + HD] for ref in both], axis=0)
            scores.append(
                lax.dot_general(
                    q_ref[:, at : at + HD],
                    k,
                    (((1,), (1,)), ((), ())),
                    preferred_element_type=F32,
                )
            )
        peaks = [jnp.max(s, axis=1, keepdims=True) for s in scores]
        for s, top in zip(scores, peaks):
            weights.append(jnp.exp2((s - top) * LOG2_SCALE))
        sums = [jnp.sum(w, axis=1, keepdims=True) for w in weights]
        for h, w, top, total in zip(heads, weights, peaks, sums):
            at = width + h * HD
            v = jnp.concatenate([ref[:, at : at + HD] for ref in both], axis=0)
            mixed = jnp.dot(w.astype(BF16), v, preferred_element_type=F32)
            out_ref[:, h * HD : (h + 1) * HD] = mixed * (1.0 / total)
            here = lanes == plane_order(h)
            tops, totals = jnp.where(here, top, tops), jnp.where(here, total, totals)
    log_ref[...] = tops * LOG2_SCALE + jnp.log2(totals)


def merge_kernel(both_ref, fresh_ref, fresh_log_ref, out_ref):
    main_ref, extra_ref = both_ref.at[:, :SUB], both_ref.at[:, SUB : 2 * SUB]
    rows = both_ref[:, 2 * SUB :].astype(F32)
    main_log = jnp.sum(rows[:, 0:3], axis=1).T[:SUB]
    extra_log = jnp.sum(rows[:, 3:6], axis=1).T[:SUB]
    fresh_log = fresh_log_ref[...]
    fresh_main, fresh_extra = fresh_log[:, :16], fresh_log[:, 16:20]

    top = jnp.maximum(main_log, fresh_main)
    a, b = jnp.exp2(main_log - top), jnp.exp2(fresh_main - top)
    scale = 1.0 / (a + b)
    a, b = a * scale, b * scale
    parts = [extra_log[:, 4 * j : 4 * j + 4] for j in range(4)] + [fresh_extra]
    top = functools.reduce(jnp.maximum, parts)
    parts = [jnp.exp2(part - top) for part in parts]
    scale = 1.0 / functools.reduce(jnp.add, parts)
    parts = [part * scale for part in parts]
    for h in range(20):
        at = h * HD
        fresh = fresh_ref[:, at : at + HD]
        n = plane_order(h)
        if n < 16:
            value = a[:, n : n + 1] * main_ref[n].astype(F32) + b[:, n : n + 1] * fresh
        else:
            g = n - 16
            value = parts[4][:, g : g + 1] * fresh
            for j in range(4):
                value += parts[j][:, g : g + 1] * extra_ref[4 * j + g].astype(F32)
        out_ref[:, at : at + HD] = value.astype(BF16)


def round_pairs(r):
    pairs = []
    for z in range(16):
        for yl in range(2):
            for yh in range(2):
                for c in range(2):
                    g, move = yh * 2 + c, (z // 2 % 2) ^ c
                    plane = 4 * ((z // 4 + (r if c == 0 else 4 - r)) % 4) + g
                    target = ((plane * 2 + (yl ^ move)) * 2 + (yh ^ move)) * 2 + z % 2
                    pairs.append(((z * 2 + yl) * 4 + g, target))
    return pairs


def per_device(fresh_q, fresh_k, fresh_v, stale_k, stale_v, scale_exps):
    z, yl, yh, c = (lax.axis_index(name) for name in ("z", "yl", "yh", "c"))
    shape = jax.ShapeDtypeStruct
    j = z // 4

    rounds = call(
        stored_kernel,
        "stored_scaled",
        [shape((PATCH * (2 if r == 0 else 1), 2 * HD), BF16) for r in range(4)],
        [SM] + [VM] * 3,
    )(jnp.stack([j, 1 + 2 * c]).astype(jnp.int32), stale_k, stale_v, scale_exps.T)
    arrived = [
        lax.ppermute(rounds[r], ("z", "yl", "yh", "c"), round_pairs(r)) for r in range(4)
    ]
    q, fresh_kv = call(
        fresh_layout_kernel,
        "fresh_layout",
        [shape((16, 2 * SUB, HD), BF16), shape((SUB, 2 * fresh_k.shape[1]), BF16)],
        [VM] * 3,
    )(fresh_q, fresh_k, fresh_v)
    arrived, q = lax.optimization_barrier((arrived, q))
    q = lax.all_to_all(q, "z", split_axis=0, concat_axis=0, tiled=True)

    shard = jnp.concatenate(arrived, axis=0)
    swap = [(0, 1), (1, 0)]
    parts = [shard] + [
        lax.ppermute(shard, ("yl", "yh"), [(i, i ^ k) for i in range(4)]) for k in (1, 2, 3)
    ]
    across_0 = lax.ppermute(shard, "c", swap)
    across_2 = lax.ppermute(parts[2], "c", swap)
    across_13 = lax.ppermute(jnp.concatenate([parts[1], parts[3]], axis=0), "c", swap)
    lows = []
    for core in (c, 1 - c):
        for k in range(4):
            source_yl, source_yh = yl ^ (k // 2), yh ^ (k % 2)
            move = source_yh ^ (z // 2 % 2)
            for r in range(4):
                patch = 4 * ((j + (4 - r) * (1 + 2 * (z % 2))) % 4) + 2 * (move ^ (z % 2)) + core
                lows.append(jnp.where(source_yl ^ move == yl, SUB * patch, -SUB))
    spans = jnp.stack([low.astype(jnp.int32) for low in lows])

    rows = shard.shape[0]
    state = attend(
        "keys_first",
        spans,
        q,
        [
            (shard, 0, 0),
            (across_0, 0, 16),
            (parts[2], 0, 8),
            (across_2, 0, 24),
            (parts[1], 0, 4),
            (parts[3], 0, 12),
        ],
    )
    (both,) = attend(
        "keys_last", spans, q, [(across_13, 0, 20), (across_13, rows, 28)], state, True
    )
    fresh_kv, both = lax.optimization_barrier((fresh_kv, both))
    fresh_far = lax.ppermute(fresh_kv, "yh", swap)
    both = lax.all_to_all(both, "z", split_axis=0, concat_axis=0, tiled=True)

    fresh_two = jnp.concatenate([fresh_kv, fresh_far], axis=0)
    fresh, fresh_log = call(
        fresh_kernel,
        "own_patch",
        [shape(fresh_q.shape, F32), shape((SUB, HD), F32)],
        [VM] * 3,
    )(fresh_q, fresh_two, lax.ppermute(fresh_two, "c", [(0, 1), (1, 0)]))

    (out,) = call(merge_kernel, "merge", [shape(fresh_q.shape, BF16)], [VM] * 3)(
        both, fresh, fresh_log
    )
    return out


def solution(mesh):
    devices = np.asarray(mesh.devices).reshape(4, 16, 2, 2, 2)
    fine = Mesh(devices, ("x", "z", "yl", "yh", "c"))
    tokens = P(("x", "z", "yl", "yh", "c"), None)
    stored = P(("x", "z", "yl"), ("yh", "c"))
    in_specs = (tokens, tokens, tokens, stored, stored, P(("x", "z", "yl"), None))
    return jax.shard_map(
        per_device, mesh=fine, in_specs=in_specs, out_specs=tokens, check_vma=False
    )
```

```python
import functools
import math

import jax
import jax.numpy as jnp
import numpy as np
from jax import lax
from jax.experimental import pallas as pl
from jax.experimental.pallas import tpu as pltpu
from jax.sharding import Mesh, PartitionSpec as P


HD = 128
LOG2_SCALE = math.log2(math.e) / math.sqrt(HD)
LOWEST = -1e30
SUB = 48
PATCH = 192
PACKED = 112
VMEM_BYTES = 24 * 2**20
VM = pl.BlockSpec(memory_space=pltpu.VMEM)
SM = pl.BlockSpec(memory_space=pltpu.SMEM)
BF16, F32 = jnp.bfloat16, jnp.float32


def call(kernel, name, outs, in_specs):
    return pl.pallas_call(
        kernel,
        out_shape=outs,
        in_specs=in_specs,
        out_specs=[VM] * len(outs),
        compiler_params=pltpu.CompilerParams(vmem_limit_bytes=VMEM_BYTES),
        name=name,
    )


def stored_kernel(first_ref, k_ref, v_ref, exps_ref, *rounds):
    scales = jnp.exp2(exps_ref[...].astype(F32))
    scales = jnp.concatenate([scales, jnp.zeros((6, PATCH), F32)], axis=0).T
    k_scale, v_scale = scales[:, 0:1], scales[:, 1:2]

    def put(ref, row, column):
        k = k_ref[:, pl.ds(column, HD)].astype(F32) * k_scale
        v = v_ref[:, pl.ds(column, HD)].astype(F32) * v_scale
        ref[row : row + PATCH, :HD] = k.astype(BF16)
        ref[row : row + PATCH, HD:] = v.astype(BF16)

    for r in range(4):
        j = (first_ref[0] + r) % 4
        put(rounds[r], 0, pl.multiple_of(j * HD, HD))
    put(rounds[0], PATCH, 4 * HD)


def fresh_layout_kernel(q_ref, fk_ref, fv_ref, q_out_ref, fresh_ref):
    for g in range(4):
        for j in range(4):
            at = (5 * g + j) * HD
            q_out_ref[4 * j + g, :SUB] = q_ref[:, at : at + HD]
            at = (5 * g + 4) * HD
            q_out_ref[4 * j + g, SUB:] = q_ref[:, at : at + HD]
    width = fk_ref.shape[1]
    fresh_ref[:, :width] = fk_ref[...]
    fresh_ref[:, width:] = fv_ref[...]


def start_state(count):
    return (
        jnp.full((1, count), LOWEST, F32),
        jnp.zeros((1, count), F32),
        jnp.zeros((HD, count), F32),
    )


def accumulate(state, queries, kv_refs, spans_ref, groups):
    top, total, acc = state
    lanes = lax.broadcasted_iota(jnp.int32, (1, queries.shape[0]), 1)
    for group in groups:
        k = jnp.concatenate([kv_refs[n][row : row + PATCH, :HD] for n, row, _ in group], axis=0)
        v = jnp.concatenate([kv_refs[n][row : row + PATCH, HD:] for n, row, _ in group], axis=0)
        s = lax.dot_general(k, queries, (((1,), (1,)), ((), ())), preferred_element_type=F32)
        blocks, masks = [], []
        new_top = top
        for n, (_, _, span) in enumerate(group):
            block = s[n * PATCH : (n + 1) * PATCH]
            low = spans_ref[span]
            mask = (lanes >= low) & (lanes < low + SUB)
            block_top = jnp.max(block, axis=0, keepdims=True)
            new_top = jnp.maximum(new_top, jnp.where(mask, LOWEST, block_top))
            blocks.append(block)
            masks.append(mask)
        shift = new_top * LOG2_SCALE
        weights = []
        shrink = jnp.exp2(top * LOG2_SCALE - shift)
        total = total * shrink
        for block, mask in zip(blocks, masks):
            w = jnp.exp2(block * LOG2_SCALE - jnp.where(mask, -LOWEST, shift))
            total = total + jnp.sum(w, axis=0, keepdims=True)
            weights.append(w.astype(BF16))
        w = jnp.concatenate(weights, axis=0)
        acc = acc * shrink + lax.dot_general(
            v, w, (((0,), (0,)), ((), ())), preferred_element_type=F32
        )
        top = new_top
    return top, total, acc


def finish(state):
    top, total, acc = state
    log_sum = top * LOG2_SCALE + jnp.log2(total)
    high = log_sum.astype(BF16).astype(F32)
    middle = (log_sum - high).astype(BF16).astype(F32)
    return (acc * (1.0 / total)).T.astype(BF16), [high, middle, log_sum - high - middle]


def queries_of(q_ref):
    count = q_ref.shape[0] * SUB
    return q_ref[:, :SUB].reshape(count, HD), q_ref[:, SUB:].reshape(count, HD)


def attend_kernel(groups, n_kv, has_state, last, spans_ref, q_ref, *refs):
    kv_refs, refs = refs[:n_kv], refs[n_kv:]
    results, rows = [], []
    for n, queries in enumerate(queries_of(q_ref)):
        if has_state:
            state = tuple(ref[...] for ref in refs[3 * n : 3 * n + 3])
        else:
            state = start_state(queries.shape[0])
        state = accumulate(state, queries, kv_refs, spans_ref, groups[n])
        if last:
            result, log_rows = finish(state)
            results.append(result)
            rows += log_rows
        else:
            for ref, value in zip(refs[6 * has_state + 3 * n :], state):
                ref[...] = value
    if not last:
        return
    out_ref = refs[-1]
    count = results[0].shape[0]
    rows = jnp.concatenate(rows + [jnp.zeros((2, count), F32)], axis=0)
    empty = jnp.zeros((8, HD), F32)
    for n in range(count // SUB):
        out_ref[n, :SUB] = results[0][n * SUB : (n + 1) * SUB]
        out_ref[n, SUB : 2 * SUB] = results[1][n * SUB : (n + 1) * SUB]
        low = min(n * SUB // HD * HD, count - 2 * HD)
        moved = rows[:, low : low + 2 * HD]
        if n * SUB > low:
            moved = pltpu.roll(moved, 2 * HD - (n * SUB - low), 1)
        moved = jnp.concatenate([moved[:, :HD], empty], axis=0)
        out_ref[n, 2 * SUB :] = moved.astype(BF16)


def attend(name, spans, q, shards, state=None, last=False):
    arrays = []
    for array, _, _ in shards:
        if not any(array is other for other in arrays):
            arrays.append(array)
    main, extra = [], []
    for array, row, span in shards:
        at = [n for n, other in enumerate(arrays) if other is array][0]
        main += [(at, row + (r + 1 if r else 0) * PATCH, span + r) for r in range(4)]
        extra.append((at, row + PATCH, span))
    groups = ([main[n : n + 12] for n in range(0, len(main), 12)], [extra])
    count = q.shape[0] * SUB
    shape = jax.ShapeDtypeStruct
    outs = [shape((1, count), F32), shape((1, count), F32), shape((HD, count), F32)] * 2
    if last:
        outs = [shape((q.shape[0], PACKED, HD), BF16)]
    state = () if state is None else tuple(state)
    kernel = functools.partial(attend_kernel, groups, len(arrays), bool(state), last)
    specs = [SM] + [VM] * (1 + len(arrays) + len(state))
    return call(kernel, name, outs, specs)(spans, q, *arrays, *state)


def plane_order(h):
    g, j = h // 5, h % 5
    return 16 + g if j == 4 else 4 * j + g


def fresh_kernel(q_ref, near_ref, far_ref, out_ref, log_ref):
    width = q_ref.shape[1]
    lanes = lax.broadcasted_iota(jnp.int32, (SUB, HD), 1)
    tops, totals = jnp.zeros((SUB, HD), F32), jnp.ones((SUB, HD), F32)
    both = (near_ref, far_ref)
    for first in range(0, width // HD, 10):
        heads = range(first, first + 10)
        scores, weights = [], []
        for h in heads:
            at = h * HD
            k = jnp.concatenate([ref[:, at : at + HD] for ref in both], axis=0)
            scores.append(
                lax.dot_general(
                    q_ref[:, at : at + HD],
                    k,
                    (((1,), (1,)), ((), ())),
                    preferred_element_type=F32,
                )
            )
        peaks = [jnp.max(s, axis=1, keepdims=True) for s in scores]
        for s, top in zip(scores, peaks):
            weights.append(jnp.exp2((s - top) * LOG2_SCALE))
        sums = [jnp.sum(w, axis=1, keepdims=True) for w in weights]
        for h, w, top, total in zip(heads, weights, peaks, sums):
            at = width + h * HD
            v = jnp.concatenate([ref[:, at : at + HD] for ref in both], axis=0)
            mixed = jnp.dot(w.astype(BF16), v, preferred_element_type=F32)
            out_ref[:, h * HD : (h + 1) * HD] = mixed * (1.0 / total)
            here = lanes == plane_order(h)
            tops, totals = jnp.where(here, top, tops), jnp.where(here, total, totals)
    log_ref[...] = tops * LOG2_SCALE + jnp.log2(totals)


def merge_kernel(both_ref, fresh_ref, fresh_log_ref, out_ref):
    main_ref, extra_ref = both_ref.at[:, :SUB], both_ref.at[:, SUB : 2 * SUB]
    rows = both_ref[:, 2 * SUB :].astype(F32)
    main_log = jnp.sum(rows[:, 0:3], axis=1).T[:SUB]
    extra_log = jnp.sum(rows[:, 3:6], axis=1).T[:SUB]
    fresh_log = fresh_log_ref[...]
    fresh_main, fresh_extra = fresh_log[:, :16], fresh_log[:, 16:20]

    top = jnp.maximum(main_log, fresh_main)
    a, b = jnp.exp2(main_log - top), jnp.exp2(fresh_main - top)
    scale = 1.0 / (a + b)
    a, b = a * scale, b * scale
    parts = [extra_log[:, 4 * j : 4 * j + 4] for j in range(4)] + [fresh_extra]
    top = functools.reduce(jnp.maximum, parts)
    parts = [jnp.exp2(part - top) for part in parts]
    scale = 1.0 / functools.reduce(jnp.add, parts)
    parts = [part * scale for part in parts]
    for h in range(20):
        at = h * HD
        fresh = fresh_ref[:, at : at + HD]
        n = plane_order(h)
        if n < 16:
            value = a[:, n : n + 1] * main_ref[n].astype(F32) + b[:, n : n + 1] * fresh
        else:
            g = n - 16
            value = parts[4][:, g : g + 1] * fresh
            for j in range(4):
                value += parts[j][:, g : g + 1] * extra_ref[4 * j + g].astype(F32)
        out_ref[:, at : at + HD] = value.astype(BF16)


def round_pairs(r):
    pairs = []
    for z in range(16):
        for yl in range(2):
            for yh in range(2):
                for c in range(2):
                    g, move = yh * 2 + c, (z // 2 % 2) ^ c
                    plane = 4 * ((z // 4 + r) % 4) + g
                    target = ((plane * 2 + (yl ^ move)) * 2 + (yh ^ move)) * 2 + z % 2
                    pairs.append(((z * 2 + yl) * 4 + g, target))
    return pairs


def per_device(fresh_q, fresh_k, fresh_v, stale_k, stale_v, scale_exps):
    z, yl, yh, c = (lax.axis_index(name) for name in ("z", "yl", "yh", "c"))
    shape = jax.ShapeDtypeStruct
    j = z // 4

    rounds = call(
        stored_kernel,
        "stored_scaled",
        [shape((PATCH * (2 if r == 0 else 1), 2 * HD), BF16) for r in range(4)],
        [SM] + [VM] * 3,
    )(j.reshape(1).astype(jnp.int32), stale_k, stale_v, scale_exps.T)
    arrived = [
        lax.ppermute(rounds[r], ("z", "yl", "yh", "c"), round_pairs(r)) for r in range(4)
    ]
    q, fresh_kv = call(
        fresh_layout_kernel,
        "fresh_layout",
        [shape((16, 2 * SUB, HD), BF16), shape((SUB, 2 * fresh_k.shape[1]), BF16)],
        [VM] * 3,
    )(fresh_q, fresh_k, fresh_v)
    arrived, q = lax.optimization_barrier((arrived, q))
    q = lax.all_to_all(q, "z", split_axis=0, concat_axis=0, tiled=True)

    shard = jnp.concatenate(arrived, axis=0)
    swap = [(0, 1), (1, 0)]
    parts = [shard] + [
        lax.ppermute(shard, ("yl", "yh"), [(i, i ^ k) for i in range(4)]) for k in (1, 2, 3)
    ]
    across_0 = lax.ppermute(shard, "c", swap)
    across_2 = lax.ppermute(parts[2], "c", swap)
    across_13 = lax.ppermute(jnp.concatenate([parts[1], parts[3]], axis=0), "c", swap)
    lows = []
    for core in (c, 1 - c):
        for k in range(4):
            source_yl, source_yh = yl ^ (k // 2), yh ^ (k % 2)
            move = source_yh ^ (z // 2 % 2)
            for r in range(4):
                patch = 4 * ((j + 4 - r) % 4) + 2 * (move ^ (z % 2)) + core
                lows.append(jnp.where(source_yl ^ move == yl, SUB * patch, -SUB))
    spans = jnp.stack([low.astype(jnp.int32) for low in lows])

    rows = shard.shape[0]
    state = attend(
        "keys_first",
        spans,
        q,
        [
            (shard, 0, 0),
            (across_0, 0, 16),
            (parts[2], 0, 8),
            (across_2, 0, 24),
            (parts[1], 0, 4),
            (parts[3], 0, 12),
        ],
    )
    (both,) = attend(
        "keys_last", spans, q, [(across_13, 0, 20), (across_13, rows, 28)], state, True
    )
    fresh_kv, both = lax.optimization_barrier((fresh_kv, both))
    fresh_far = lax.ppermute(fresh_kv, "yh", swap)
    both = lax.all_to_all(both, "z", split_axis=0, concat_axis=0, tiled=True)

    fresh_two = jnp.concatenate([fresh_kv, fresh_far], axis=0)
    fresh, fresh_log = call(
        fresh_kernel,
        "own_patch",
        [shape(fresh_q.shape, F32), shape((SUB, HD), F32)],
        [VM] * 3,
    )(fresh_q, fresh_two, lax.ppermute(fresh_two, "c", [(0, 1), (1, 0)]))

    (out,) = call(merge_kernel, "merge", [shape(fresh_q.shape, BF16)], [VM] * 3)(
        both, fresh, fresh_log
    )
    return out


def solution(mesh):
    devices = np.asarray(mesh.devices).reshape(4, 16, 2, 2, 2)
    fine = Mesh(devices, ("x", "z", "yl", "yh", "c"))
    tokens = P(("x", "z", "yl", "yh", "c"), None)
    stored = P(("x", "z", "yl"), ("yh", "c"))
    in_specs = (tokens, tokens, tokens, stored, stored, P(("x", "z", "yl"), None))
    return jax.shard_map(
        per_device, mesh=fine, in_specs=in_specs, out_specs=tokens, check_vma=False
    )
```
